32 devices in a mesh: groups: 2 (over x), pool: 8 (over z, y), tp: 2 (over core).
Axes of the slice: x: 2, y: 2, z: 4, core: 2. Of those that a mesh axis runs over, the one named last changes fastest.
Arguments:
- q_lat: bfloat16 [2048, 64, 512], P(('groups', 'pool'), 'tp'), parts along dimension 0, may hold values from -8 to 8
- q_rope: bfloat16 [2048, 4096], P(('groups', 'pool'), 'tp'), parts along dimension 0, may hold values from -80 to 80
- new_lat: bfloat16 [2048, 512], P(('groups', 'pool')), parts along dimension 0, may hold values from -6 to 6
- new_rope: bfloat16 [2048, 64], P(('groups', 'pool')), parts along dimension 0, may hold values from -24 to 24
- pool_lat: bfloat16 [256, 64, 512], P(('groups', 'pool')), parts along dimension 0, may hold values from -6 to 6
- pool_rope: bfloat16 [256, 4096], P(('groups', 'pool')), parts along dimension 0, may hold values from -6 to 6
- hit_block: int32 [96], P(('groups', 'pool')), parts along dimension 0, may hold values from 0 to 15
- hit_owner: int32 [96, 1], P(('groups', 'pool')), parts along dimension 0, may hold values from 0 to 7; in each aligned block of 6 rows (0 to 5, 6 to 11, ...) at most 2 rows name the same one
- suffix_len: int32 [16], P(('groups', 'pool')), parts along dimension 0, may hold values from 1 to 128, 768 in all
- new_place: int32 [32], P(('groups', 'pool')), parts along dimension 0, may hold values from 0 to 15, each once
- w_uv: bfloat16 [64, 512, 128], P('tp'), may hold values from -0.5 to 0.5
Outputs:
- attn_out: bfloat16 [2048, 8192], P(('groups', 'pool'), 'tp'), parts along dimension 0
- written_lat: bfloat16 [32, 64, 512], P(('groups', 'pool')), parts along dimension 0
- written_rope: bfloat16 [32, 4096], P(('groups', 'pool')), parts along dimension 0
The draws below stay inside these ranges and needn't reach their ends.
There are 2 independent parts, one for each index of `groups`. The reference program is written for one: setup_inputs(seed, part) draws one part's arguments, and reference() takes and returns one part's arrays. A program takes and returns all parts, laid end to end along the dimension named above; an argument that names none is the same for every part. Nothing has to cross between parts.
Inputs may be any that keep to these rules, and one draw needn't show every extreme that they name: `hit_owner`: among the 6 hits of one request no owner is named more than 2 times, a bound that some block reaches. `suffix_len`: some request of a group has exactly 128 live tokens. `new_place`: every new block is named exactly once.
All inputs are finite; a program needn't handle non-finite values.
Results may differ from the reference program's by a relative error of at most 0.0058.
Values may be sent and summed in bfloat16 or wider, within the bound.
No kernel may reach another device: no remote copies, remote signals or barrier semaphores. Data moves between devices by JAX's collectives and lax.ppermute only.
A program may use at most 128 MiB of HBM per device.

```python
import math
import jax
import jax.numpy as jnp
import numpy as np
from jax import lax

HEADS = 64
LATENT = 512
ROPE = 64
VHEAD = 128
BLOCK = 64
CAP = 2
SUF = 128
POOL_BLK = 16
HIT = 6
TOKENS = 1024
HITS = 48
BLOCKS = 128
NEWS = 16
N_POOL = 8


def draw_new_rope(key, part):
    key = jax.random.fold_in(key, 11)
    values = jnp.clip(jax.random.normal(key, (N_POOL, SUF, ROPE), jnp.float32), -6.0, 6.0)
    return values.reshape(TOKENS, ROPE).astype(jnp.bfloat16)


def draw_q_rope(key, part):
    key = jax.random.fold_in(key, 12)
    values = jnp.clip(jax.random.normal(key, (N_POOL, SUF, HEADS, ROPE), jnp.float32), -6.0, 6.0)
    return values.reshape(TOKENS, HEADS * ROPE).astype(jnp.bfloat16)


def touch_ends(drawn, rng, least, largest):
    spot = [jax.random.randint(jax.random.fold_in(rng, axis), (), 0, length) for axis, length in enumerate(drawn.shape)]
    main_axis = drawn.shape.index(max(drawn.shape))
    neighbour = spot[:main_axis] + [(spot[main_axis] + 1) % drawn.shape[main_axis]] + spot[main_axis + 1:]
    return drawn.at[tuple(spot)].set(least).at[tuple(neighbour)].set(largest)


def levels(key, dims, pieces, least, largest):
    factor_of, own = 1.0, jax.random.fold_in(key, 6)
    for axis_at, parts in pieces:
        draws = jnp.exp(jax.random.uniform(jax.random.fold_in(own, axis_at), (parts,), jnp.float32, least / len(pieces), largest / len(pieces)))
        factor_of = factor_of * jnp.repeat(draws, dims[axis_at] // parts).reshape([-1 if axis == axis_at else 1 for axis in range(len(dims))])
    return factor_of


def split_up(number_of, total, limit, skew):
    loads = [(1 << 20) // math.isqrt(rank ** skew) + 1 for rank in range(2, number_of + 1)]
    surplus, given = total - limit - (number_of - 1), [1] * (number_of - 1)
    while surplus > 0:
        movable = [i for i in range(number_of - 1) if given[i] < limit]
        whole, left = sum([loads[i] for i in movable]), surplus
        for i in movable:
            extra = min(limit - given[i], max(1, left * loads[i] // whole), surplus)
            given[i] = given[i] + extra
            surplus = surplus - extra
    return np.array([limit] + given)


def ragged(own_key, number_of, total, limit, skew):
    if number_of == 2:
        one = jax.random.randint(own_key, (), max(1, total - limit), min(limit, total - 1) + 1)
        return jnp.stack([one, total - one])
    tallies = jnp.asarray(split_up(number_of, total, limit, skew), jnp.int32)
    twos = (number_of - 1) // 2
    giver, sink = tallies[1:1 + 2 * twos:2], tallies[2:2 + 2 * twos:2]
    slack = jnp.minimum(giver - 1, limit - sink)
    moved = jax.random.randint(jax.random.fold_in(own_key, 1), (twos,), 0, 1 << 20) % (slack + 1)
    tallies = tallies.at[1:1 + 2 * twos:2].set(giver - moved).at[2:2 + 2 * twos:2].set(sink + moved)
    return tallies[jax.random.permutation(jax.random.fold_in(own_key, 2), number_of)]


def deal_out(own_key, own, number, rows, amount, top, most, slope):
    order = jax.random.permutation(own_key, amount)
    heavy_load, ordinary = load_shares(amount, rows * top, most, slope, True), load_shares(amount, rows * top, most, slope, False)
    places = jnp.arange(amount)

    def named(tallies, turn):
        used = int((tallies > 0).sum())
        fixed = max(1, used // 4)
        moved = fixed + (places - fixed + turn * (used - fixed)) % max(1, amount - fixed)
        return jnp.zeros((amount,), jnp.int32).at[order[jnp.where(places < fixed, places, moved)]].set(jnp.asarray(tallies, jnp.int32))

    tallies = jnp.where(number % 4 == 0, named(heavy_load, number // 4), named(ordinary, number - number // 4 - 1))
    mixed = jax.random.permutation(jax.random.fold_in(own, 3), amount)
    donor, taker = mixed[0:amount // 2 * 2:2], mixed[1:amount // 2 * 2:2]
    room = jnp.minimum(tallies[donor] - 1, most - tallies[taker]) // 2
    room = jnp.where((donor == order[0]) | (taker == order[0]) | (tallies[taker] == 0), 0, jnp.maximum(room, 0))
    moved = jax.random.randint(jax.random.fold_in(own, 4), (amount // 2,), 0, 1 << 20) % (room + 1)
    tallies = tallies.at[donor].add(-moved).at[taker].add(moved)
    items = jnp.searchsorted(jnp.cumsum(tallies), jnp.arange(rows * top), side="right").astype(jnp.int32)
    listing = items.reshape(top, rows).T
    listing = listing[jax.random.permutation(jax.random.fold_in(own, 1), rows)]
    turn = jax.random.randint(jax.random.fold_in(own, 2), (rows, 1), 0, top)
    return jnp.take_along_axis(listing, (jnp.arange(top)[None, :] + turn) % top, axis=1)


def load_shares(amount, total, limit, lean, full):
    weights = [(1 << 20) // math.isqrt(grade ** lean) + 1 for grade in range(1, amount + 1)]
    largest = limit if full else min(limit, max(-(-total // amount), total * weights[0] // sum(weights)))
    least = 1 if total - largest >= amount - 1 else 0
    given, spare = [largest] + [least] * (amount - 1), total - largest - least * (amount - 1)
    while spare > 0:
        free = [i for i in range(1, amount) if given[i] < largest] or [i for i in range(1, amount) if given[i] < limit]
        mass, remaining = sum([weights[i] for i in free]), spare
        for i in free:
            more = min(limit - given[i], max(1, remaining * weights[i] // mass), spare)
            given[i] = given[i] + more
            spare = spare - more
    return np.array(given)


def noise(key, shape, deviation, reach, pieces=(), dtype=jnp.bfloat16):
    values = deviation * jax.random.normal(key, shape, jnp.float32)
    if pieces:
        values = values * levels(key, shape, pieces, -0.22, 0.18)
    return jnp.clip(values, -reach, reach).astype(dtype)


def setup_inputs(seed: int = 0, part: int = 0) -> dict:
    arg_keys = jax.random.split(jax.random.key(seed), 12)
    part_splits = jax.random.split(jax.random.fold_in(arg_keys[11], part), 12)
    q_lat = noise(part_splits[0], (TOKENS, HEADS, LATENT), 1.5, 8.0, ((0, 8), (1, 2)))
    q_rope = draw_q_rope(jax.random.fold_in(jax.random.fold_in(arg_keys[11], part), 71), part)
    new_lat = noise(part_splits[2], (TOKENS, LATENT), 1.0, 6.0, ((0, 8),))
    new_rope = draw_new_rope(jax.random.fold_in(jax.random.fold_in(arg_keys[11], part), 71), part)
    pool_lat = noise(part_splits[4], (BLOCKS, BLOCK, LATENT), 1.0, 6.0, ((0, 8),))
    pool_rope = noise(part_splits[5], (BLOCKS, BLOCK * ROPE), 1.0, 6.0, ((0, 8),))
    hit_block = touch_ends(jax.random.randint(part_splits[6], (HITS,), 0, POOL_BLK), jax.random.fold_in(part_splits[6], 1), 0, POOL_BLK - 1).astype(jnp.int32)
    hit_owner_keys = jax.random.split(jax.random.fold_in(part_splits[7], 1), HITS // HIT)
    hit_owner_turns = jax.random.permutation(jax.random.fold_in(part_splits[7], 3), HITS // HIT)
    hit_owner = jax.vmap(lambda own, number: deal_out(jax.random.fold_in(part_splits[7], 2), own, number, HIT, N_POOL, 1, CAP, 2))(hit_owner_keys, hit_owner_turns).reshape((HITS, 1))
    suffix_len = ragged(part_splits[8], N_POOL, N_POOL * SUF * 3 // 4, SUF, 1).astype(jnp.int32)
    new_place = jax.random.permutation(part_splits[9], NEWS).astype(jnp.int32)
    w_uv = noise(arg_keys[10], (HEADS, LATENT, VHEAD), (LATENT // 4) ** -0.5, 0.5, ((0, 2),))
    return {"q_lat": q_lat, "q_rope": q_rope, "new_lat": new_lat, "new_rope": new_rope, "pool_lat": pool_lat, "pool_rope": pool_rope, "hit_block": hit_block, "hit_owner": hit_owner, "suffix_len": suffix_len, "new_place": new_place, "w_uv": w_uv}


softmax_scale = 1.0 / math.sqrt(192.0)

def reference(q_lat, q_rope, new_lat, new_rope, pool_lat, pool_rope, hit_block, hit_owner, suffix_len, new_place, w_uv):
    query_lat = q_lat.reshape(N_POOL, SUF, HEADS, LATENT)
    query_rope = q_rope.reshape(N_POOL, SUF, HEADS, ROPE)
    suffix_lat = new_lat.reshape(N_POOL, SUF, LATENT)
    suffix_rope = new_rope.reshape(N_POOL, SUF, ROPE)
    block_ids = (hit_owner[:, 0] * POOL_BLK + hit_block).astype(jnp.int32).reshape(N_POOL, HIT)
    up_weight = w_uv.astype(jnp.float32)
    prefix_len = HIT * BLOCK

    def one_request(inputs):
        row_qlat, row_qrope, row_lat, row_rope, row_ids, length = inputs
        prefix_lat = pool_lat[row_ids].reshape(prefix_len, LATENT)
        prefix_rope = pool_rope[row_ids].reshape(prefix_len, ROPE)
        keys_lat = jnp.concatenate([prefix_lat, row_lat], axis=0).astype(jnp.float32)
        keys_rope = jnp.concatenate([prefix_rope, row_rope], axis=0).astype(jnp.float32)
        scores = jnp.einsum('shl,kl->shk', row_qlat.astype(jnp.float32), keys_lat)
        scores = scores + jnp.einsum('shr,kr->shk', row_qrope.astype(jnp.float32), keys_rope)
        scores = scores * softmax_scale
        positions = lax.iota(jnp.int32, SUF)
        key_pos = lax.iota(jnp.int32, prefix_len + SUF)
        allowed = (key_pos[None, :] < prefix_len) | (key_pos[None, :] - prefix_len <= positions[:, None])
        scores = jnp.where(allowed[:, None, :], scores, -1e+30)
        weights = jax.nn.softmax(scores, axis=-1).astype(jnp.bfloat16)
        weights = lax.optimization_barrier(weights)
        context = jnp.einsum('shk,kl->shl', weights.astype(jnp.float32), keys_lat).astype(jnp.bfloat16)
        context = lax.optimization_barrier(context)
        result = jnp.einsum('shl,hlv->shv', context.astype(jnp.float32), up_weight)
        result = jnp.where((positions < length)[:, None, None], result, 0.0)
        return result.astype(jnp.bfloat16).reshape(SUF, HEADS * VHEAD)
    attn_out = lax.map(one_request, (query_lat, query_rope, suffix_lat, suffix_rope, block_ids, suffix_len))
    attn_out = attn_out.reshape(TOKENS, HEADS * VHEAD)
    live_rows = lax.iota(jnp.int32, SUF)[None, :] < suffix_len[:, None]
    masked_lat = jnp.where(live_rows[:, :, None], suffix_lat, jnp.zeros_like(suffix_lat)).reshape(NEWS, BLOCK, LATENT)
    masked_rope = jnp.where(live_rows[:, :, None], suffix_rope, jnp.zeros_like(suffix_rope)).reshape(NEWS, BLOCK * ROPE)
    written_lat = masked_lat[new_place]
    written_rope = masked_rope[new_place]
    return (attn_out, written_lat, written_rope)
```

```python
import functools
import math

import jax
import jax.numpy as jnp
from jax import lax
from jax.experimental import pallas as pl
from jax.experimental.pallas import tpu as pltpu
from jax.sharding import PartitionSpec as P

CAP = 2
LANES = 128
softmax_scale = 1.0 / math.sqrt(192.0)
exp2_scale = softmax_scale / math.log(2.0)


def gather_kernel(hits, asks, pool_ref, out_ref, sem):
    me = lax.axis_index("pool")
    peers = out_ref.shape[0]

    def each_request(fn):
        def body(r, carry):
            rank = jnp.int32(0)
            for k in range(hits):
                mine = asks[r, k] == me

                @pl.when(mine)
                def _(rank=rank, k=k):
                    fn(r, rank, asks[r, hits + k])

                rank = rank + mine.astype(jnp.int32)
            return carry

        lax.fori_loop(0, peers, body, 0)

    def copy(r, rank, block):
        slot = jnp.minimum(rank, CAP - 1)
        return pltpu.make_async_copy(pool_ref.at[block], out_ref.at[r, slot], sem)

    each_request(lambda r, rank, block: copy(r, rank, block).start())
    each_request(lambda r, rank, block: copy(r, rank, block).wait())


def attend_kernel(
    block_len,
    owners,
    length,
    own_ref,
    sib_ref,
    new_lat_ref,
    new_rope_ref,
    q_ref,
    qr_ref,
    w_ref,
    out_ref,
    keys,
    rope,
):
    hits = owners.shape[0]
    group, rows, latent = q_ref.shape
    rope_width = qr_ref.shape[2]
    half = block_len // 2
    quarter = half // 2
    prefix = hits * block_len
    total = prefix + rows
    tiles = latent // LANES

    @pl.when(pl.program_id(0) == 0)
    def _():
        for k in range(hits):
            owner = owners[k]
            rank = jnp.int32(0)
            for j in range(k):
                rank = rank + (owners[j] == owner).astype(jnp.int32)
            for side, ref in enumerate((own_ref, sib_ref)):
                block = ref.at[owner, jnp.minimum(rank, CAP - 1)]
                base = k * block_len + side * half
                for t in range(tiles):
                    keys[base : base + half, t * LANES : (t + 1) * LANES] = block[
                        t * half : (t + 1) * half, :
                    ]
                packed = block[tiles * half : tiles * half + quarter, :]
                rope[base : base + quarter, :] = packed[:, :rope_width]
                rope[base + quarter : base + half, :] = packed[:, rope_width:]
        keys[prefix:, :] = new_lat_ref[...]
        rope[prefix:, :] = new_rope_ref[...]

    contract = (((1,), (1,)), ((), ()))
    q = q_ref[...].reshape(group * rows, latent)
    qr = qr_ref[...].reshape(group * rows, rope_width)
    scores = lax.dot_general(q, keys[...], contract, preferred_element_type=jnp.float32)
    scores = scores + lax.dot_general(
        qr, rope[...], contract, preferred_element_type=jnp.float32
    )
    position = lax.broadcasted_iota(jnp.int32, (group, rows, rows), 1).reshape(group * rows, rows)
    key_at = lax.broadcasted_iota(jnp.int32, (group * rows, rows), 1)
    tail = jnp.where(key_at <= position, scores[:, prefix:], -1e30)
    scores = jnp.concatenate([scores[:, :prefix], tail], axis=1)
    top = jnp.max(scores, axis=1, keepdims=True)
    parts = jnp.exp2((scores - top) * exp2_scale)
    norm = 1.0 / jnp.sum(parts, axis=1, keepdims=True)
    weights = (parts * norm).astype(jnp.bfloat16)
    context = jnp.dot(weights, keys[...], preferred_element_type=jnp.float32).astype(jnp.bfloat16)
    width = w_ref.shape[2]
    live = lax.broadcasted_iota(jnp.int32, (rows, width), 0) < length[0]
    for g in range(group):
        result = jnp.dot(
            context[g * rows : (g + 1) * rows], w_ref[g], preferred_element_type=jnp.float32
        )
        out_ref[:, g * width : (g + 1) * width] = jnp.where(live, result, 0.0).astype(
            out_ref.dtype
        )


def local(
    q_lat,
    q_rope,
    new_lat,
    new_rope,
    pool_lat,
    pool_rope,
    hit_block,
    hit_owner,
    suffix_len,
    new_place,
    w_uv,
):
    peers = lax.axis_size("pool")
    me = lax.axis_index("pool")
    core = lax.axis_index("tp")
    cores = lax.axis_size("tp")
    assert cores == 2
    hits = hit_block.shape[0]
    blocks, block_len, latent = pool_lat.shape
    rows, rope_width = new_rope.shape
    half = block_len // 2
    quarter = half // 2
    tiles = latent // LANES
    heads = q_lat.shape[1]
    vhead = w_uv.shape[2]
    new_count = rows // block_len
    swap = [(0, 1), (1, 0)]

    owners = hit_owner[:, 0]
    ask = jnp.pad(jnp.concatenate([owners, hit_block]), (0, LANES - 2 * hits))
    ask = jnp.broadcast_to(ask[None, :], (peers, LANES))
    asks = lax.all_to_all(ask, "pool", split_axis=0, concat_axis=0, tiled=True)

    lat_half = lax.dynamic_slice_in_dim(pool_lat, core * half, half, axis=1)
    lat_half = lat_half.reshape(blocks, half, tiles, LANES).transpose(0, 2, 1, 3)
    rope_half = lax.dynamic_slice_in_dim(
        pool_rope, core * half * rope_width, half * rope_width, axis=1
    )
    rope_half = rope_half.reshape(blocks, 2, quarter, rope_width).transpose(0, 2, 1, 3)
    cached = jnp.concatenate(
        [
            lat_half.reshape(blocks, tiles * half, LANES),
            rope_half.reshape(blocks, quarter, 2 * rope_width),
        ],
        axis=1,
    )
    depth = cached.shape[1]

    found = pl.pallas_call(
        functools.partial(gather_kernel, hits),
        grid_spec=pltpu.PrefetchScalarGridSpec(
            num_scalar_prefetch=1,
            grid=(1,),
            in_specs=[pl.BlockSpec(memory_space=pl.ANY)],
            out_specs=pl.BlockSpec(memory_space=pl.ANY),
            scratch_shapes=[pltpu.SemaphoreType.DMA],
        ),
        out_shape=jax.ShapeDtypeStruct((peers, CAP, depth, LANES), cached.dtype),
        name="gather_hits",
    )(asks, cached)
    own = lax.all_to_all(found, "pool", split_axis=0, concat_axis=0, tiled=True)
    sib = lax.ppermute(own, "tp", swap)

    length = suffix_len[0]
    live = lax.iota(jnp.int32, rows) < length
    mine_lat = jnp.where(live[:, None], new_lat, jnp.zeros_like(new_lat))
    mine_rope = jnp.where(live[:, None], new_rope, jnp.zeros_like(new_rope))
    mine_lat = mine_lat.reshape(new_count, 2, half, latent)
    mine_lat = lax.dynamic_index_in_dim(mine_lat, core, axis=1, keepdims=False)
    rope_rows = half * rope_width // latent
    mine_rope = mine_rope.reshape(new_count, 2, rope_rows, latent)
    mine_rope = lax.dynamic_index_in_dim(mine_rope, core, axis=1, keepdims=False)
    every = jnp.concatenate([mine_lat, mine_rope], axis=1)
    source = new_place // new_count
    differs = source ^ me
    place = jnp.zeros_like(source)
    bit = peers // 2
    step = 0
    while bit:
        other = lax.ppermute(every, "pool", [(i, i ^ bit) for i in range(peers)])
        every = jnp.concatenate([every, other], axis=0)
        place = place + ((differs & bit) != 0).astype(jnp.int32) * (1 << step)
        bit //= 2
        step += 1
    chosen = every[place * new_count + new_place % new_count]
    chosen_sib = lax.ppermute(chosen, "tp", swap)
    first = jnp.where(core == 0, chosen, chosen_sib)
    second = jnp.where(core == 0, chosen_sib, chosen)
    written_lat = jnp.concatenate([first[:, :half], second[:, :half]], axis=1)
    written_rope = jnp.concatenate([first[:, half:], second[:, half:]], axis=1).reshape(
        new_place.shape[0], block_len * rope_width
    )

    q_heads = q_lat.transpose(1, 0, 2)
    qr_heads = q_rope.reshape(rows, heads, rope_width).transpose(1, 0, 2)
    group = 4
    total = hits * block_len + rows
    whole = pl.BlockSpec(memory_space=pltpu.VMEM)
    flops = 2 * heads * rows * (total * (2 * latent + rope_width) + latent * vhead)
    attn_out = pl.pallas_call(
        functools.partial(attend_kernel, block_len),
        grid_spec=pltpu.PrefetchScalarGridSpec(
            num_scalar_prefetch=2,
            grid=(heads // group,),
            in_specs=[
                whole,
                whole,
                whole,
                whole,
                pl.BlockSpec((group, rows, latent), lambda i, *_: (i, 0, 0)),
                pl.BlockSpec((group, rows, rope_width), lambda i, *_: (i, 0, 0)),
                pl.BlockSpec((group, latent, vhead), lambda i, *_: (i, 0, 0)),
            ],
            out_specs=pl.BlockSpec((rows, group * vhead), lambda i, *_: (0, i)),
            scratch_shapes=[
                pltpu.VMEM((total, latent), jnp.bfloat16),
                pltpu.VMEM((total, rope_width), jnp.bfloat16),
            ],
        ),
        out_shape=jax.ShapeDtypeStruct((rows, heads * vhead), jnp.bfloat16),
        compiler_params=pltpu.CompilerParams(vmem_limit_bytes=40 * 1024 * 1024),
        cost_estimate=pl.CostEstimate(
            flops=flops, bytes_accessed=10 * 2**20, transcendentals=heads * rows * total
        ),
        name="attend",
    )(owners, suffix_len, own, sib, new_lat, new_rope, q_heads, qr_heads, w_uv)
    return (attn_out, written_lat, written_rope)


def solution(mesh):
    return jax.shard_map(
        local,
        mesh=mesh,
        in_specs=(
            P(("groups", "pool"), "tp", None),
            P(("groups", "pool"), "tp"),
            P(("groups", "pool"), None),
            P(("groups", "pool"), None),
            P(("groups", "pool"), None, None),
            P(("groups", "pool"), None),
            P(("groups", "pool")),
            P(("groups", "pool"), None),
            P(("groups", "pool")),
            P(("groups", "pool")),
            P("tp", None, None),
        ),
        out_specs=(
            P(("groups", "pool"), "tp"),
            P(("groups", "pool"), None, None),
            P(("groups", "pool"), None),
        ),
        check_vma=False,
    )
```

```python
import functools
import math

import jax
import jax.numpy as jnp
from jax import lax
from jax.experimental import pallas as pl
from jax.experimental.pallas import tpu as pltpu
from jax.sharding import PartitionSpec as P

CAP = 2
LANES = 128
softmax_scale = 1.0 / math.sqrt(192.0)
exp2_scale = softmax_scale / math.log(2.0)


def gather_kernel(hits, asks, pool_ref, out_ref):
    me = lax.axis_index("pool")

    def body(r, carry):
        rank = jnp.int32(0)
        wanted = [jnp.int32(0)] * CAP
        for k in range(hits):
            mine = (asks[r, k] == me).astype(jnp.int32)
            for s in range(CAP):
                wanted[s] = jnp.where((rank == s) & (mine == 1), asks[r, hits + k], wanted[s])
            rank = rank + mine
        for s in range(CAP):
            out_ref[r, s] = pool_ref[wanted[s]]
        return carry

    lax.fori_loop(0, out_ref.shape[0], body, 0)


def attend_kernel(
    block_len,
    owners,
    length,
    own_ref,
    sib_ref,
    new_lat_ref,
    new_rope_ref,
    q_ref,
    qr_ref,
    w_ref,
    out_ref,
    keys,
    rope,
):
    hits = owners.shape[0]
    group, rows, latent = q_ref.shape
    rope_width = qr_ref.shape[2]
    half = block_len // 2
    quarter = half // 2
    prefix = hits * block_len
    total = prefix + rows
    tiles = latent // LANES

    @pl.when(pl.program_id(0) == 0)
    def _():
        for k in range(hits):
            owner = owners[k]
            rank = jnp.int32(0)
            for j in range(k):
                rank = rank + (owners[j] == owner).astype(jnp.int32)
            for side, ref in enumerate((own_ref, sib_ref)):
                block = ref.at[owner, jnp.minimum(rank, CAP - 1)]
                base = k * block_len + side * half
                for t in range(tiles):
                    keys[base : base + half, t * LANES : (t + 1) * LANES] = block[
                        t * half : (t + 1) * half, :
                    ]
                packed = block[tiles * half : tiles * half + quarter, :]
                rope[base : base + quarter, :] = packed[:, :rope_width]
                rope[base + quarter : base + half, :] = packed[:, rope_width:]
        keys[prefix:, :] = new_lat_ref[...]
        rope[prefix:, :] = new_rope_ref[...]

    contract = (((1,), (1,)), ((), ()))
    q = q_ref[...].reshape(group * rows, latent)
    qr = qr_ref[...].reshape(group * rows, rope_width)
    scores = lax.dot_general(q, keys[...], contract, preferred_element_type=jnp.float32)
    scores = scores + lax.dot_general(
        qr, rope[...], contract, preferred_element_type=jnp.float32
    )
    position = lax.broadcasted_iota(jnp.int32, (group, rows, rows), 1).reshape(group * rows, rows)
    key_at = lax.broadcasted_iota(jnp.int32, (group * rows, rows), 1)
    tail = jnp.where(key_at <= position, scores[:, prefix:], -1e30)
    scores = jnp.concatenate([scores[:, :prefix], tail], axis=1)
    top = jnp.max(scores, axis=1, keepdims=True)
    parts = jnp.exp2((scores - top) * exp2_scale)
    norm = 1.0 / jnp.sum(parts, axis=1, keepdims=True)
    weights = (parts * norm).astype(jnp.bfloat16)
    context = jnp.dot(weights, keys[...], preferred_element_type=jnp.float32).astype(jnp.bfloat16)
    width = w_ref.shape[2]
    live = lax.broadcasted_iota(jnp.int32, (rows, width), 0) < length[0]
    for g in range(group):
        result = jnp.dot(
            context[g * rows : (g + 1) * rows], w_ref[g], preferred_element_type=jnp.float32
        )
        out_ref[:, g * width : (g + 1) * width] = jnp.where(live, result, 0.0).astype(
            out_ref.dtype
        )


def local(
    q_lat,
    q_rope,
    new_lat,
    new_rope,
    pool_lat,
    pool_rope,
    hit_block,
    hit_owner,
    suffix_len,
    new_place,
    w_uv,
):
    peers = lax.axis_size("pool")
    me = lax.axis_index("pool")
    core = lax.axis_index("tp")
    cores = lax.axis_size("tp")
    assert cores == 2
    hits = hit_block.shape[0]
    blocks, block_len, latent = pool_lat.shape
    rows, rope_width = new_rope.shape
    half = block_len // 2
    quarter = half // 2
    tiles = latent // LANES
    heads = q_lat.shape[1]
    vhead = w_uv.shape[2]
    new_count = rows // block_len
    swap = [(0, 1), (1, 0)]

    owners = hit_owner[:, 0]
    ask = jnp.pad(jnp.concatenate([owners, hit_block]), (0, LANES - 2 * hits))
    ask = jnp.broadcast_to(ask[None, :], (peers, LANES))
    asks = lax.all_to_all(ask, "pool", split_axis=0, concat_axis=0, tiled=True)

    lat_half = lax.dynamic_slice_in_dim(pool_lat, core * half, half, axis=1)
    lat_half = lat_half.reshape(blocks, half, tiles, LANES).transpose(0, 2, 1, 3)
    rope_half = lax.dynamic_slice_in_dim(
        pool_rope, core * half * rope_width, half * rope_width, axis=1
    )
    rope_half = rope_half.reshape(blocks, 2, quarter, rope_width).transpose(0, 2, 1, 3)
    cached = jnp.concatenate(
        [
            lat_half.reshape(blocks, tiles * half, LANES),
            rope_half.reshape(blocks, quarter, 2 * rope_width),
        ],
        axis=1,
    )
    depth = cached.shape[1]

    length = suffix_len[0]
    live = lax.iota(jnp.int32, rows) < length
    mine_lat = jnp.where(live[:, None], new_lat, jnp.zeros_like(new_lat))
    mine_rope = jnp.where(live[:, None], new_rope, jnp.zeros_like(new_rope))
    mine_lat = mine_lat.reshape(new_count, 2, half, latent)
    mine_lat = lax.dynamic_index_in_dim(mine_lat, core, axis=1, keepdims=False)
    rope_rows = half * rope_width // latent
    mine_rope = mine_rope.reshape(new_count, 2, rope_rows, latent)
    mine_rope = lax.dynamic_index_in_dim(mine_rope, core, axis=1, keepdims=False)
    every = jnp.concatenate([mine_lat, mine_rope], axis=1)
    bit = peers // 2
    other = lax.ppermute(every, "pool", [(i, i ^ bit) for i in range(peers)])
    asks, every, other = lax.optimization_barrier((asks, every, other))
    every = jnp.concatenate([every, other], axis=0)

    found = pl.pallas_call(
        functools.partial(gather_kernel, hits),
        grid_spec=pltpu.PrefetchScalarGridSpec(
            num_scalar_prefetch=1,
            grid=(1,),
            in_specs=[pl.BlockSpec(memory_space=pltpu.VMEM)],
            out_specs=pl.BlockSpec(memory_space=pltpu.VMEM),
        ),
        out_shape=jax.ShapeDtypeStruct((peers, CAP, depth, LANES), cached.dtype),
        compiler_params=pltpu.CompilerParams(vmem_limit_bytes=16 * 1024 * 1024),
        name="gather_hits",
    )(asks, cached)
    own = lax.all_to_all(found, "pool", split_axis=0, concat_axis=0, tiled=True)
    q_heads = q_lat.transpose(1, 0, 2)
    qr_heads = q_rope.reshape(rows, heads, rope_width).transpose(1, 0, 2)
    own, q_heads, qr_heads = lax.optimization_barrier((own, q_heads, qr_heads))
    sib = lax.ppermute(own, "tp", swap)

    source = new_place // new_count
    differs = source ^ me
    place = ((differs & bit) != 0).astype(jnp.int32)
    bit //= 2
    step = 1
    while bit:
        other = lax.ppermute(every, "pool", [(i, i ^ bit) for i in range(peers)])
        every = jnp.concatenate([every, other], axis=0)
        place = place + ((differs & bit) != 0).astype(jnp.int32) * (1 << step)
        bit //= 2
        step += 1
    chosen = every[place * new_count + new_place % new_count]
    chosen_sib = lax.ppermute(chosen, "tp", swap)
    first = jnp.where(core == 0, chosen, chosen_sib)
    second = jnp.where(core == 0, chosen_sib, chosen)
    written_lat = jnp.concatenate([first[:, :half], second[:, :half]], axis=1)
    written_rope = jnp.concatenate([first[:, half:], second[:, half:]], axis=1).reshape(
        new_place.shape[0], block_len * rope_width
    )

    group = 4
    total = hits * block_len + rows
    whole = pl.BlockSpec(memory_space=pltpu.VMEM)
    flops = 2 * heads * rows * (total * (2 * latent + rope_width) + latent * vhead)
    attn_out = pl.pallas_call(
        functools.partial(attend_kernel, block_len),
        grid_spec=pltpu.PrefetchScalarGridSpec(
            num_scalar_prefetch=2,
            grid=(heads // group,),
            in_specs=[
                whole,
                whole,
                whole,
                whole,
                pl.BlockSpec((group, rows, latent), lambda i, *_: (i, 0, 0)),
                pl.BlockSpec((group, rows, rope_width), lambda i, *_: (i, 0, 0)),
                pl.BlockSpec((group, latent, vhead), lambda i, *_: (i, 0, 0)),
            ],
            out_specs=pl.BlockSpec((rows, group * vhead), lambda i, *_: (0, i)),
            scratch_shapes=[
                pltpu.VMEM((total, latent), jnp.bfloat16),
                pltpu.VMEM((total, rope_width), jnp.bfloat16),
            ],
        ),
        out_shape=jax.ShapeDtypeStruct((rows, heads * vhead), jnp.bfloat16),
        compiler_params=pltpu.CompilerParams(vmem_limit_bytes=60 * 1024 * 1024),
        cost_estimate=pl.CostEstimate(
            flops=flops, bytes_accessed=10 * 2**20, transcendentals=heads * rows * total
        ),
        name="attend",
    )(owners, suffix_len, own, sib, new_lat, new_rope, q_heads, qr_heads, w_uv)
    return (attn_out, written_lat, written_rope)


def solution(mesh):
    return jax.shard_map(
        local,
        mesh=mesh,
        in_specs=(
            P(("groups", "pool"), "tp", None),
            P(("groups", "pool"), "tp"),
            P(("groups", "pool"), None),
            P(("groups", "pool"), None),
            P(("groups", "pool"), None, None),
            P(("groups", "pool"), None),
            P(("groups", "pool")),
            P(("groups", "pool"), None),
            P(("groups", "pool")),
            P(("groups", "pool")),
            P("tp", None, None),
        ),
        out_specs=(
            P(("groups", "pool"), "tp"),
            P(("groups", "pool"), None, None),
            P(("groups", "pool"), None),
        ),
        check_vma=False,
    )
```

```python
import functools
import math

import jax
import jax.numpy as jnp
from jax import lax
from jax.experimental import pallas as pl
from jax.experimental.pallas import tpu as pltpu
from jax.sharding import PartitionSpec as P

CAP = 2
LANES = 128
softmax_scale = 1.0 / math.sqrt(192.0)
exp2_scale = softmax_scale / math.log(2.0)


def gather_kernel(hits, asks, pool_ref, out_ref):
    me = lax.axis_index("pool")

    def body(r, carry):
        rank = jnp.int32(0)
        wanted = [jnp.int32(0)] * CAP
        for k in range(hits):
            mine = (asks[r, k] == me).astype(jnp.int32)
            for s in range(CAP):
                wanted[s] = jnp.where((rank == s) & (mine == 1), asks[r, hits + k], wanted[s])
            rank = rank + mine
        for s in range(CAP):
            out_ref[r, s] = pool_ref[wanted[s]]
        return carry

    lax.fori_loop(0, out_ref.shape[0], body, 0)


def ask_kernel(block_len, *refs):
    sources, out_ref, held = refs[:6], refs[6], refs[7:13]
    tokens, rows32, sems = refs[13:]
    copies = [
        pltpu.make_async_copy(source, dest, sems.at[i])
        for i, (source, dest) in enumerate(zip(sources, held))
    ]
    for copy in copies:
        copy.start()
    for copy in copies:
        copy.wait()
    hit_block, hit_owner, length, new_place, lat_ref, rope_ref = held
    core = lax.axis_index("tp")
    pieces = out_ref.shape[0]
    latent = lat_ref.shape[1]
    tiles = latent // LANES
    half = block_len // 2
    part = half // (pieces // tiles)
    new_count = lat_ref.shape[0] // block_len
    hits = hit_block.shape[0]
    pairs = half // 2 // pieces

    lane = lax.broadcasted_iota(jnp.int32, (1, LANES), 1)
    ask = jnp.zeros((1, LANES), jnp.int32)
    for k in range(hits):
        ask = jnp.where(lane == k, hit_owner[k], ask)
        ask = jnp.where(lane == hits + k, hit_block[k], ask)
    for s in range(new_count):
        ask = jnp.where(lane == 2 * hits + s, new_place[s], ask)
    ask = ask.astype(jnp.float32)

    token_keep = lax.broadcasted_iota(jnp.int32, tokens.shape, 0) < length[0]
    tokens[...] = jnp.where(token_keep, rope_ref[...].astype(jnp.float32).T, 0.0)
    for b in range(new_count):
        base = b * block_len + core * half
        at = pl.multiple_of(base, half)
        keep = lax.broadcasted_iota(jnp.int32, (half, latent), 0) + base < length[0]
        lat = jnp.where(keep, lat_ref[pl.ds(at, half), :].astype(jnp.float32), 0.0)
        lat = lat.astype(out_ref.dtype)
        for j in range(pieces):
            u, t = j // tiles, j % tiles
            out_ref[j, b * part : (b + 1) * part, :] = lat[
                u * part : (u + 1) * part, t * LANES : (t + 1) * LANES
            ]
        even = tokens[pl.ds(at, half // 2, stride=2), :]
        odd = tokens[pl.ds(at + 1, half // 2, stride=2), :]
        paired = jnp.concatenate([even, odd], axis=1)
        for j in range(pieces):
            for p in range(pairs):
                row = p * new_count + b
                g = j * pairs + p
                rows32[j, row : row + 1, :] = paired[g : g + 1]
    filled = pairs * new_count
    for j in range(pieces):
        rows32[j, filled:8, :] = jnp.zeros((8 - filled, LANES), jnp.float32)
        rows32[j, 8:16, :] = jnp.broadcast_to(ask, (8, LANES))
        out_ref[j, new_count * part :, :] = rows32[j].astype(out_ref.dtype)


def answer_kernel(hits, new_count, asks_ref, pool_ref, out_ref, rows32, ids_vec, ids, sem):
    me = lax.axis_index("pool")
    peers, depth = out_ref.shape[0], pool_ref.shape[1]
    tail = asks_ref.shape[1] - 16
    part = tail // new_count
    for r in range(peers):
        tile = asks_ref[r, tail:, :].astype(jnp.float32)
        rows32[r] = tile
        ids_vec[r : r + 1, :] = tile[8:9].astype(jnp.int32)
    copy = pltpu.make_async_copy(ids_vec, ids, sem)
    copy.start()
    copy.wait()
    pairs_row = lax.broadcasted_iota(jnp.int32, (8, LANES), 0)

    def body(r, carry):
        rank = jnp.int32(0)
        wanted = [jnp.int32(0)] * CAP
        for k in range(hits):
            mine = (ids[r, k] == me).astype(jnp.int32)
            for s in range(CAP):
                wanted[s] = jnp.where((rank == s) & (mine == 1), ids[r, hits + k], wanted[s])
            rank = rank + mine
        for s in range(CAP):
            out_ref[r, s * depth : (s + 1) * depth, :] = pool_ref[wanted[s]]
        base = CAP * depth
        merged = jnp.zeros((8, LANES), jnp.float32)
        for s in range(new_count):
            place = ids[r, 2 * hits + s]
            source, block = place // new_count, place % new_count
            out_ref[r, base + s * part : base + (s + 1) * part, :] = asks_ref[
                source, pl.ds(pl.multiple_of(block * part, part), part), :
            ]
            tile = rows32[source, 0:8, :]
            shifted = tile
            for move in range(1, new_count):
                up = pltpu.roll(tile, 8 - move, 0)
                down = pltpu.roll(tile, move, 0)
                shifted = jnp.where(block - s == move, up, shifted)
                shifted = jnp.where(s - block == move, down, shifted)
            merged = jnp.where(pairs_row % new_count == s, shifted, merged)
        both = jnp.concatenate([merged, jnp.zeros((8, LANES), jnp.float32)], axis=0)
        out_ref[r, base + tail :, :] = both.astype(out_ref.dtype)
        return carry

    lax.fori_loop(0, peers, body, 0)


def write_back(block_len, base, own_ref, sib_ref, lat_ref, rope_ref):
    core = lax.axis_index("tp")
    pieces = own_ref.shape[0]
    slots, _, latent = lat_ref.shape
    tiles = latent // LANES
    half = block_len // 2
    part = half // (pieces // tiles)
    pairs = half // 2 // pieces
    sides = []
    for side, ref in enumerate((own_ref, sib_ref)):
        start = pl.multiple_of((core if side == 0 else 1 - core) * half, half)
        row = []
        for j in range(pieces):
            u, t = j // tiles, j % tiles
            for s in range(slots):
                lat_ref[s, pl.ds(start + u * part, part), t * LANES : (t + 1) * LANES] = ref[
                    j, base + s * part : base + (s + 1) * part, :
                ]
            tile = ref[j, base + slots * part :, :].astype(jnp.float32)
            for p in range(pairs):
                row.append(tile[p * slots : (p + 1) * slots])
        sides.append(jnp.concatenate(row, axis=1))
    first = jnp.where(core == 0, sides[0], sides[1])
    second = jnp.where(core == 0, sides[1], sides[0])
    rope_ref[...] = jnp.concatenate([first, second], axis=1).astype(rope_ref.dtype)


def suffix_kernel(group, lat_ref, rope_ref, *refs):
    sources, (out_ref, done_ref), held, sems = refs[:2], refs[2:4], refs[4:6], refs[6]
    q_ref, qr_ref = held
    heads, rows, latent = q_ref.shape
    steps = heads // group

    def arrive(g, a):
        at = pl.ds(g * group, group)
        return pltpu.make_async_copy(sources[a].at[at], held[a].at[at], sems.at[g, a])

    for g in range(steps):
        arrive(g, 0).start()
        arrive(g, 1).start()
    position = lax.broadcasted_iota(jnp.int32, (group, rows, rows), 1)
    key_at = lax.broadcasted_iota(jnp.int32, (group, rows, rows), 2)
    for g in range(steps):
        arrive(g, 0).wait()
        arrive(g, 1).wait()
        at = slice(g * group, (g + 1) * group)
        q = q_ref[at].reshape(group * rows, latent)
        qr = qr_ref[at].reshape(group * rows, qr_ref.shape[2])
        scores = lax.dot_general(
            q, lat_ref[...], (((1,), (1,)), ((), ())), preferred_element_type=jnp.float32
        )
        scores = scores + jnp.dot(qr, rope_ref[...], preferred_element_type=jnp.float32)
        out_ref[at] = jnp.where(key_at <= position, scores.reshape(group, rows, rows), -1e30)
    done_ref[...] = jnp.zeros_like(done_ref)


def attend_kernel(
    block_len, owners, length, own_ref, sib_ref, done_ref, new_lat_ref, q_ref, qr_ref, tail_ref, w_ref, *refs
):
    out_ref, *written = refs[:-2]
    keys, rope = refs[-2:]
    hits = owners.shape[0]
    group, rows, latent = q_ref.shape
    rope_width = qr_ref.shape[2]
    width = w_ref.shape[2]
    half = block_len // 2
    quarter = half // 2
    prefix = hits * block_len
    tiles = latent // LANES
    depth = tiles * half + quarter

    @pl.when(pl.program_id(0) == 0)
    def _():
        for k in range(hits):
            owner = owners[k]
            rank = jnp.int32(0)
            for j in range(k):
                rank = rank + (owners[j] == owner).astype(jnp.int32)
            slot = pl.multiple_of(jnp.minimum(rank, CAP - 1) * depth, 16)
            for side, ref in enumerate((own_ref, sib_ref)):
                block = ref.at[owner, pl.ds(slot, depth), :]
                base = k * block_len + side * half
                for t in range(tiles):
                    keys[base : base + half, t * LANES : (t + 1) * LANES] = block[
                        t * half : (t + 1) * half, :
                    ]
                packed = block[tiles * half : tiles * half + quarter, :]
                rope[base : base + quarter, :] = packed[:, :rope_width]
                rope[base + quarter : base + half, :] = packed[:, rope_width:]
        keys[prefix:, :] = new_lat_ref[...]
        if written:
            write_back(block_len, depth * CAP, own_ref, sib_ref, *written)

    contract = (((1,), (1,)), ((), ()))
    live = lax.broadcasted_iota(jnp.int32, (rows, width), 0) < length[0]
    q = q_ref[...].reshape(group * rows, latent)
    qr = qr_ref[...].reshape(group * rows, rope_width)
    scores = lax.dot_general(q, keys[:prefix, :], contract, preferred_element_type=jnp.float32)
    scores = scores + lax.dot_general(
        qr, rope[...], contract, preferred_element_type=jnp.float32
    )
    scores = jnp.concatenate([scores, tail_ref[...].reshape(group * rows, rows)], axis=1)
    top = jnp.max(scores, axis=1, keepdims=True)
    parts = jnp.exp2((scores - top) * exp2_scale)
    norm = 1.0 / jnp.sum(parts, axis=1, keepdims=True)
    weights = (parts * norm).astype(jnp.bfloat16)
    context = jnp.dot(weights, keys[...], preferred_element_type=jnp.float32)
    context = context.astype(jnp.bfloat16)
    for h in range(group):
        value = jnp.dot(
            context[h * rows : (h + 1) * rows], w_ref[h], preferred_element_type=jnp.float32
        )
        out_ref[:, h * width : (h + 1) * width] = jnp.where(live, value, 0.0).astype(
            out_ref.dtype
        )


def local(
    q_lat,
    q_rope,
    new_lat,
    new_rope,
    pool_lat,
    pool_rope,
    hit_block,
    hit_owner,
    suffix_len,
    new_place,
    w_uv,
):
    peers = lax.axis_size("pool")
    me = lax.axis_index("pool")
    core = lax.axis_index("tp")
    cores = lax.axis_size("tp")
    assert cores == 2
    hits = hit_block.shape[0]
    blocks, block_len, latent = pool_lat.shape
    rows, rope_width = new_rope.shape
    half = block_len // 2
    quarter = half // 2
    tiles = latent // LANES
    heads = q_lat.shape[1]
    vhead = w_uv.shape[2]
    new_count = rows // block_len
    swap = [(0, 1), (1, 0)]

    owners = hit_owner[:, 0]
    whole = pl.BlockSpec(memory_space=pltpu.VMEM)
    anywhere = pl.BlockSpec(memory_space=pl.ANY)
    part = half * tiles // peers
    two_hops = peers % tiles == 0 and part % 16 == 0 and half % (2 * peers) == 0

    lat_half = lax.dynamic_slice_in_dim(pool_lat, core * half, half, axis=1)
    lat_half = lat_half.reshape(blocks, half, tiles, LANES).transpose(0, 2, 1, 3)
    rope_half = lax.dynamic_slice_in_dim(
        pool_rope, core * half * rope_width, half * rope_width, axis=1
    )
    rope_half = rope_half.reshape(blocks, 2, quarter, rope_width).transpose(0, 2, 1, 3)
    cached = jnp.concatenate(
        [
            lat_half.reshape(blocks, tiles * half, LANES),
            rope_half.reshape(blocks, quarter, 2 * rope_width),
        ],
        axis=1,
    )
    depth = cached.shape[1]

    if two_hops:
        asked = pl.pallas_call(
            functools.partial(ask_kernel, block_len),
            in_specs=[anywhere] * 6,
            out_specs=whole,
            scratch_shapes=[
                pltpu.SMEM((hits,), jnp.int32),
                pltpu.SMEM((hits,), jnp.int32),
                pltpu.SMEM((1,), jnp.int32),
                pltpu.SMEM(new_place.shape, jnp.int32),
                pltpu.VMEM((rows, latent), new_lat.dtype),
                pltpu.VMEM((rope_width, rows), new_rope.dtype),
                pltpu.VMEM((rows, rope_width), jnp.float32),
                pltpu.VMEM((peers, 16, LANES), jnp.float32),
                pltpu.SemaphoreType.DMA((6,)),
            ],
            out_shape=jax.ShapeDtypeStruct((peers, new_count * part + 16, LANES), new_lat.dtype),
            compiler_params=pltpu.CompilerParams(vmem_limit_bytes=60 * 1024 * 1024),
            name="ask",
        )(hit_block, owners, suffix_len, new_place, new_lat, new_rope.T)
        asks = lax.all_to_all(asked, "pool", split_axis=0, concat_axis=0, tiled=True)
        found = pl.pallas_call(
            functools.partial(answer_kernel, hits, new_count),
            in_specs=[whole] * 2,
            out_specs=whole,
            scratch_shapes=[
                pltpu.VMEM((peers, 16, LANES), jnp.float32),
                pltpu.VMEM((peers, LANES), jnp.int32),
                pltpu.SMEM((peers, LANES), jnp.int32),
                pltpu.SemaphoreType.DMA,
            ],
            out_shape=jax.ShapeDtypeStruct(
                (peers, CAP * depth + new_count * part + 16, LANES), cached.dtype
            ),
            compiler_params=pltpu.CompilerParams(vmem_limit_bytes=8 * 1024 * 1024),
            name="answer",
        )(asks, cached)
        own = lax.all_to_all(found, "pool", split_axis=0, concat_axis=0, tiled=True)
    else:
        ask = jnp.pad(jnp.concatenate([owners, hit_block]), (0, LANES - 2 * hits))
        ask = jnp.broadcast_to(ask[None, :], (peers, LANES))
        asks = lax.all_to_all(ask, "pool", split_axis=0, concat_axis=0, tiled=True)

        length = suffix_len[0]
        live = lax.iota(jnp.int32, rows) < length
        mine_lat = jnp.where(live[:, None], new_lat, jnp.zeros_like(new_lat))
        mine_rope = jnp.where(live[:, None], new_rope, jnp.zeros_like(new_rope))
        mine_lat = mine_lat.reshape(new_count, 2, half, latent)
        mine_lat = lax.dynamic_index_in_dim(mine_lat, core, axis=1, keepdims=False)
        rope_rows = half * rope_width // latent
        mine_rope = mine_rope.reshape(new_count, 2, rope_rows, latent)
        mine_rope = lax.dynamic_index_in_dim(mine_rope, core, axis=1, keepdims=False)
        every = jnp.concatenate([mine_lat, mine_rope], axis=1)
        bit = peers // 2
        other = lax.ppermute(every, "pool", [(i, i ^ bit) for i in range(peers)])
        asks, every, other = lax.optimization_barrier((asks, every, other))
        every = jnp.concatenate([every, other], axis=0)

        found = pl.pallas_call(
            functools.partial(gather_kernel, hits),
            grid_spec=pltpu.PrefetchScalarGridSpec(
                num_scalar_prefetch=1,
                grid=(1,),
                in_specs=[pl.BlockSpec(memory_space=pltpu.VMEM)],
                out_specs=pl.BlockSpec(memory_space=pltpu.VMEM),
            ),
            out_shape=jax.ShapeDtypeStruct((peers, CAP, depth, LANES), cached.dtype),
            compiler_params=pltpu.CompilerParams(vmem_limit_bytes=16 * 1024 * 1024),
            name="gather_hits",
        )(asks, cached)
        found = found.reshape(peers, CAP * depth, LANES)
        own = lax.all_to_all(found, "pool", split_axis=0, concat_axis=0, tiled=True)
    q_heads = q_lat.transpose(1, 0, 2)
    qr_heads = q_rope.reshape(rows, heads, rope_width).transpose(1, 0, 2)
    group = 8
    tail, done = pl.pallas_call(
        functools.partial(suffix_kernel, group),
        in_specs=[whole] * 2 + [anywhere] * 2,
        out_specs=[whole] * 2,
        out_shape=[
            jax.ShapeDtypeStruct((heads, rows, rows), jnp.float32),
            jax.ShapeDtypeStruct((8, LANES), jnp.float32),
        ],
        scratch_shapes=[
            pltpu.VMEM(q_heads.shape, q_heads.dtype),
            pltpu.VMEM(qr_heads.shape, qr_heads.dtype),
            pltpu.SemaphoreType.DMA((heads // group, 2)),
        ],
        compiler_params=pltpu.CompilerParams(vmem_limit_bytes=58 * 1024 * 1024),
        cost_estimate=pl.CostEstimate(
            flops=2 * heads * rows * rows * (latent + rope_width),
            bytes_accessed=12 * 2**20,
            transcendentals=0,
        ),
        name="suffix",
    )(new_lat, new_rope.T, q_heads, qr_heads)
    own, done = lax.optimization_barrier((own, done))
    sib = lax.ppermute(own, "tp", swap)
    if not two_hops:
        source = new_place // new_count
        differs = source ^ me
        place = ((differs & bit) != 0).astype(jnp.int32)
        bit //= 2
        step = 1
        while bit:
            other = lax.ppermute(every, "pool", [(i, i ^ bit) for i in range(peers)])
            every = jnp.concatenate([every, other], axis=0)
            place = place + ((differs & bit) != 0).astype(jnp.int32) * (1 << step)
            bit //= 2
            step += 1
        chosen = every[place * new_count + new_place % new_count]
        chosen_sib = lax.ppermute(chosen, "tp", swap)
        first = jnp.where(core == 0, chosen, chosen_sib)
        second = jnp.where(core == 0, chosen_sib, chosen)
        written_lat = jnp.concatenate([first[:, :half], second[:, :half]], axis=1)
        written_rope = jnp.concatenate([first[:, half:], second[:, half:]], axis=1).reshape(
            new_place.shape[0], block_len * rope_width
        )

    total = hits * block_len + rows
    flops = 2 * heads * rows * (total * (2 * latent + rope_width) + latent * vhead)
    out_specs = [pl.BlockSpec((rows, group * vhead), lambda i, *_: (0, i))]
    out_shape = [jax.ShapeDtypeStruct((rows, heads * vhead), jnp.bfloat16)]
    if two_hops:
        slots = new_place.shape[0]
        for shape in ((slots, block_len, latent), (slots, block_len * rope_width)):
            out_specs.append(whole)
            out_shape.append(jax.ShapeDtypeStruct(shape, new_lat.dtype))
    streamed = [
        pl.BlockSpec((group,) + x.shape[1:], lambda i, *_: (i, 0, 0))
        for x in (q_heads, qr_heads, tail, w_uv)
    ]
    attn_out, *written = pl.pallas_call(
        functools.partial(attend_kernel, block_len),
        grid_spec=pltpu.PrefetchScalarGridSpec(
            num_scalar_prefetch=2,
            grid=(heads // group,),
            in_specs=[whole] * 4 + streamed,
            out_specs=out_specs,
            scratch_shapes=[
                pltpu.VMEM((total, latent), jnp.bfloat16),
                pltpu.VMEM((hits * block_len, rope_width), jnp.bfloat16),
            ],
        ),
        out_shape=out_shape,
        compiler_params=pltpu.CompilerParams(vmem_limit_bytes=60 * 1024 * 1024),
        cost_estimate=pl.CostEstimate(
            flops=flops, bytes_accessed=10 * 2**20, transcendentals=heads * rows * total
        ),
        name="attend",
    )(owners, suffix_len, own, sib, done, new_lat, q_heads, qr_heads, tail, w_uv)
    if two_hops:
        written_lat, written_rope = written
    return (attn_out, written_lat, written_rope)


def solution(mesh):
    return jax.shard_map(
        local,
        mesh=mesh,
        in_specs=(
            P(("groups", "pool"), "tp", None),
            P(("groups", "pool"), "tp"),
            P(("groups", "pool"), None),
            P(("groups", "pool"), None),
            P(("groups", "pool"), None, None),
            P(("groups", "pool"), None),
            P(("groups", "pool")),
            P(("groups", "pool"), None),
            P(("groups", "pool")),
            P(("groups", "pool")),
            P("tp", None, None),
        ),
        out_specs=(
            P(("groups", "pool"), "tp"),
            P(("groups", "pool"), None, None),
            P(("groups", "pool"), None),
        ),
        check_vma=False,
    )
```

```python
import functools
import math

import jax
import jax.numpy as jnp
from jax import lax
from jax.experimental import pallas as pl
from jax.experimental.pallas import tpu as pltpu
from jax.sharding import PartitionSpec as P

CAP = 2
LANES = 128
softmax_scale = 1.0 / math.sqrt(192.0)
exp2_scale = softmax_scale / math.log(2.0)


def gather_kernel(hits, asks, pool_ref, out_ref):
    me = lax.axis_index("pool")

    def body(r, carry):
        rank = jnp.int32(0)
        wanted = [jnp.int32(0)] * CAP
        for k in range(hits):
            mine = (asks[r, k] == me).astype(jnp.int32)
            for s in range(CAP):
                wanted[s] = jnp.where((rank == s) & (mine == 1), asks[r, hits + k], wanted[s])
            rank = rank + mine
        for s in range(CAP):
            out_ref[r, s] = pool_ref[wanted[s]]
        return carry

    lax.fori_loop(0, out_ref.shape[0], body, 0)


def ask_kernel(block_len, *refs):
    sources, out_ref, held = refs[:6], refs[6], refs[7:13]
    tokens, rows32, sems = refs[13:]
    copies = [
        pltpu.make_async_copy(source, dest, sems.at[i])
        for i, (source, dest) in enumerate(zip(sources, held))
    ]
    for copy in copies:
        copy.start()
    for copy in copies:
        copy.wait()
    hit_block, hit_owner, length, new_place, lat_ref, rope_ref = held
    core = lax.axis_index("tp")
    pieces = out_ref.shape[0]
    latent = lat_ref.shape[1]
    tiles = latent // LANES
    half = block_len // 2
    part = half // (pieces // tiles)
    new_count = lat_ref.shape[0] // block_len
    hits = hit_block.shape[0]
    pairs = half // 2 // pieces

    lane = lax.broadcasted_iota(jnp.int32, (1, LANES), 1)
    ask = jnp.zeros((1, LANES), jnp.int32)
    for k in range(hits):
        ask = jnp.where(lane == k, hit_owner[k], ask)
        ask = jnp.where(lane == hits + k, hit_block[k], ask)
    for s in range(new_count):
        ask = jnp.where(lane == 2 * hits + s, new_place[s], ask)
    ask = ask.astype(jnp.float32)

    token_keep = lax.broadcasted_iota(jnp.int32, tokens.shape, 0) < length[0]
    tokens[...] = jnp.where(token_keep, rope_ref[...].astype(jnp.float32).T, 0.0)
    for b in range(new_count):
        base = b * block_len + core * half
        at = pl.multiple_of(base, half)
        keep = lax.broadcasted_iota(jnp.int32, (half, latent), 0) + base < length[0]
        lat = jnp.where(keep, lat_ref[pl.ds(at, half), :].astype(jnp.float32), 0.0)
        lat = lat.astype(out_ref.dtype)
        for j in range(pieces):
            u, t = j // tiles, j % tiles
            out_ref[j, b * part : (b + 1) * part, :] = lat[
                u * part : (u + 1) * part, t * LANES : (t + 1) * LANES
            ]
        even = tokens[pl.ds(at, half // 2, stride=2), :]
        odd = tokens[pl.ds(at + 1, half // 2, stride=2), :]
        paired = jnp.concatenate([even, odd], axis=1)
        for j in range(pieces):
            for p in range(pairs):
                row = p * new_count + b
                g = j * pairs + p
                rows32[j, row : row + 1, :] = paired[g : g + 1]
    filled = pairs * new_count
    for j in range(pieces):
        rows32[j, filled:8, :] = jnp.zeros((8 - filled, LANES), jnp.float32)
        rows32[j, 8:16, :] = jnp.broadcast_to(ask, (8, LANES))
        out_ref[j, new_count * part :, :] = rows32[j].astype(out_ref.dtype)


def answer_kernel(hits, new_count, asks_ref, pool_ref, out_ref, rows32, ids_vec, ids, sem):
    me = lax.axis_index("pool")
    peers, depth = out_ref.shape[0], pool_ref.shape[1]
    tail = asks_ref.shape[1] - 16
    part = tail // new_count
    for r in range(peers):
        tile = asks_ref[r, tail:, :].astype(jnp.float32)
        rows32[r] = tile
        ids_vec[r : r + 1, :] = tile[8:9].astype(jnp.int32)
    copy = pltpu.make_async_copy(ids_vec, ids, sem)
    copy.start()
    copy.wait()
    pairs_row = lax.broadcasted_iota(jnp.int32, (8, LANES), 0)

    def body(r, carry):
        rank = jnp.int32(0)
        wanted = [jnp.int32(0)] * CAP
        for k in range(hits):
            mine = (ids[r, k] == me).astype(jnp.int32)
            for s in range(CAP):
                wanted[s] = jnp.where((rank == s) & (mine == 1), ids[r, hits + k], wanted[s])
            rank = rank + mine
        for s in range(CAP):
            out_ref[r, s * depth : (s + 1) * depth, :] = pool_ref[wanted[s]]
        base = CAP * depth
        merged = jnp.zeros((8, LANES), jnp.float32)
        for s in range(new_count):
            place = ids[r, 2 * hits + s]
            source, block = place // new_count, place % new_count
            out_ref[r, base + s * part : base + (s + 1) * part, :] = asks_ref[
                source, pl.ds(pl.multiple_of(block * part, part), part), :
            ]
            tile = rows32[source, 0:8, :]
            shifted = tile
            for move in range(1, new_count):
                up = pltpu.roll(tile, 8 - move, 0)
                down = pltpu.roll(tile, move, 0)
                shifted = jnp.where(block - s == move, up, shifted)
                shifted = jnp.where(s - block == move, down, shifted)
            merged = jnp.where(pairs_row % new_count == s, shifted, merged)
        both = jnp.concatenate([merged, jnp.zeros((8, LANES), jnp.float32)], axis=0)
        out_ref[r, base + tail :, :] = both.astype(out_ref.dtype)
        return carry

    lax.fori_loop(0, peers, body, 0)


def write_back(block_len, base, own_ref, sib_ref, lat_ref, rope_ref):
    core = lax.axis_index("tp")
    pieces = own_ref.shape[0]
    slots, _, latent = lat_ref.shape
    tiles = latent // LANES
    half = block_len // 2
    part = half // (pieces // tiles)
    pairs = half // 2 // pieces
    sides = []
    for side, ref in enumerate((own_ref, sib_ref)):
        start = pl.multiple_of((core if side == 0 else 1 - core) * half, half)
        row = []
        for j in range(pieces):
            u, t = j // tiles, j % tiles
            for s in range(slots):
                lat_ref[s, pl.ds(start + u * part, part), t * LANES : (t + 1) * LANES] = ref[
                    j, base + s * part : base + (s + 1) * part, :
                ]
            tile = ref[j, base + slots * part :, :].astype(jnp.float32)
            for p in range(pairs):
                row.append(tile[p * slots : (p + 1) * slots])
        sides.append(jnp.concatenate(row, axis=1))
    first = jnp.where(core == 0, sides[0], sides[1])
    second = jnp.where(core == 0, sides[1], sides[0])
    rope_ref[...] = jnp.concatenate([first, second], axis=1).astype(rope_ref.dtype)


def suffix_kernel(group, lat_ref, rope_ref, *refs):
    sources, out_ref, held, sems = refs[:2], refs[2], refs[3:5], refs[5]
    q_ref, qr_ref = held
    heads, rows, latent = q_ref.shape
    steps = heads // group

    def arrive(g, a):
        at = pl.ds(g * group, group)
        return pltpu.make_async_copy(sources[a].at[at], held[a].at[at], sems.at[g, a])

    for g in range(steps):
        arrive(g, 0).start()
        arrive(g, 1).start()
    position = lax.broadcasted_iota(jnp.int32, (group, rows, rows), 1)
    key_at = lax.broadcasted_iota(jnp.int32, (group, rows, rows), 2)
    for g in range(steps):
        arrive(g, 0).wait()
        arrive(g, 1).wait()
        at = slice(g * group, (g + 1) * group)
        q = q_ref[at].reshape(group * rows, latent)
        qr = qr_ref[at].reshape(group * rows, qr_ref.shape[2])
        scores = lax.dot_general(
            q, lat_ref[...], (((1,), (1,)), ((), ())), preferred_element_type=jnp.float32
        )
        scores = scores + jnp.dot(qr, rope_ref[...], preferred_element_type=jnp.float32)
        out_ref[at] = jnp.where(key_at <= position, scores.reshape(group, rows, rows), -1e30)


def attend_kernel(
    block_len, hits, numbers, own_ref, sib_ref, new_lat_ref, q_ref, qr_ref, tail_ref, w_ref, *refs
):
    out_ref, *written = refs[:-2]
    keys, rope = refs[-2:]
    group, rows, latent = q_ref.shape
    rope_width = qr_ref.shape[2]
    width = w_ref.shape[2]
    half = block_len // 2
    quarter = half // 2
    prefix = hits * block_len
    tiles = latent // LANES
    depth = tiles * half + quarter

    @pl.when(pl.program_id(0) == 0)
    def _():
        for k in range(hits):
            owner = numbers[k]
            rank = jnp.int32(0)
            for j in range(k):
                rank = rank + (numbers[j] == owner).astype(jnp.int32)
            slot = pl.multiple_of(jnp.minimum(rank, CAP - 1) * depth, 16)
            for side, ref in enumerate((own_ref, sib_ref)):
                block = ref.at[owner, pl.ds(slot, depth), :]
                base = k * block_len + side * half
                for t in range(tiles):
                    keys[base : base + half, t * LANES : (t + 1) * LANES] = block[
                        t * half : (t + 1) * half, :
                    ]
                packed = block[tiles * half : tiles * half + quarter, :]
                rope[base : base + quarter, :] = packed[:, :rope_width]
                rope[base + quarter : base + half, :] = packed[:, rope_width:]
        keys[prefix:, :] = new_lat_ref[...]
        if written:
            write_back(block_len, depth * CAP, own_ref, sib_ref, *written)

    contract = (((1,), (1,)), ((), ()))
    live = lax.broadcasted_iota(jnp.int32, (rows, width), 0) < numbers[hits]
    some = 4

    def score(i):
        at = slice(i * some, (i + 1) * some)
        q = q_ref[at].reshape(some * rows, latent)
        qr = qr_ref[at].reshape(some * rows, rope_width)
        scores = lax.dot_general(q, keys[:prefix, :], contract, preferred_element_type=jnp.float32)
        scores = scores + lax.dot_general(
            qr, rope[...], contract, preferred_element_type=jnp.float32
        )
        return jnp.concatenate([scores, tail_ref[at].reshape(some * rows, rows)], axis=1)

    def finish(i, scores):
        top = jnp.max(scores, axis=1, keepdims=True)
        parts = jnp.exp2((scores - top) * exp2_scale)
        norm = 1.0 / jnp.sum(parts, axis=1, keepdims=True)
        weights = (parts * norm).astype(jnp.bfloat16)
        context = jnp.dot(weights, keys[...], preferred_element_type=jnp.float32)
        context = context.astype(jnp.bfloat16)
        for h in range(some):
            value = jnp.dot(
                context[h * rows : (h + 1) * rows],
                w_ref[i * some + h],
                preferred_element_type=jnp.float32,
            )
            lanes = slice((i * some + h) * width, (i * some + h + 1) * width)
            out_ref[:, lanes] = jnp.where(live, value, 0.0).astype(out_ref.dtype)

    scores = score(0)
    for i in range(group // some):
        later = score(i + 1) if (i + 1) * some < group else None
        finish(i, scores)
        scores = later


def local(
    q_lat,
    q_rope,
    new_lat,
    new_rope,
    pool_lat,
    pool_rope,
    hit_block,
    hit_owner,
    suffix_len,
    new_place,
    w_uv,
):
    peers = lax.axis_size("pool")
    me = lax.axis_index("pool")
    core = lax.axis_index("tp")
    cores = lax.axis_size("tp")
    assert cores == 2
    hits = hit_block.shape[0]
    blocks, block_len, latent = pool_lat.shape
    rows, rope_width = new_rope.shape
    half = block_len // 2
    quarter = half // 2
    tiles = latent // LANES
    heads = q_lat.shape[1]
    vhead = w_uv.shape[2]
    new_count = rows // block_len
    swap = [(0, 1), (1, 0)]

    owners = hit_owner[:, 0]
    whole = pl.BlockSpec(memory_space=pltpu.VMEM)
    anywhere = pl.BlockSpec(memory_space=pl.ANY)
    part = half * tiles // peers
    two_hops = peers % tiles == 0 and part % 16 == 0 and half % (2 * peers) == 0

    lat_half = lax.dynamic_slice_in_dim(pool_lat, core * half, half, axis=1)
    lat_half = lat_half.reshape(blocks, half, tiles, LANES).transpose(0, 2, 1, 3)
    rope_half = lax.dynamic_slice_in_dim(
        pool_rope, core * half * rope_width, half * rope_width, axis=1
    )
    rope_half = rope_half.reshape(blocks, 2, quarter, rope_width).transpose(0, 2, 1, 3)
    cached = jnp.concatenate(
        [
            lat_half.reshape(blocks, tiles * half, LANES),
            rope_half.reshape(blocks, quarter, 2 * rope_width),
        ],
        axis=1,
    )
    depth = cached.shape[1]

    if two_hops:
        asked = pl.pallas_call(
            functools.partial(ask_kernel, block_len),
            in_specs=[anywhere] * 6,
            out_specs=whole,
            scratch_shapes=[
                pltpu.SMEM((hits,), jnp.int32),
                pltpu.SMEM((hits,), jnp.int32),
                pltpu.SMEM((1,), jnp.int32),
                pltpu.SMEM(new_place.shape, jnp.int32),
                pltpu.VMEM((rows, latent), new_lat.dtype),
                pltpu.VMEM((rope_width, rows), new_rope.dtype),
                pltpu.VMEM((rows, rope_width), jnp.float32),
                pltpu.VMEM((peers, 16, LANES), jnp.float32),
                pltpu.SemaphoreType.DMA((6,)),
            ],
            out_shape=jax.ShapeDtypeStruct((peers, new_count * part + 16, LANES), new_lat.dtype),
            compiler_params=pltpu.CompilerParams(vmem_limit_bytes=60 * 1024 * 1024),
            name="ask",
        )(hit_block, owners, suffix_len, new_place, new_lat, new_rope.T)
        asks = lax.all_to_all(asked, "pool", split_axis=0, concat_axis=0, tiled=True)
        found = pl.pallas_call(
            functools.partial(answer_kernel, hits, new_count),
            in_specs=[whole] * 2,
            out_specs=whole,
            scratch_shapes=[
                pltpu.VMEM((peers, 16, LANES), jnp.float32),
                pltpu.VMEM((peers, LANES), jnp.int32),
                pltpu.SMEM((peers, LANES), jnp.int32),
                pltpu.SemaphoreType.DMA,
            ],
            out_shape=jax.ShapeDtypeStruct(
                (peers, CAP * depth + new_count * part + 16, LANES), cached.dtype
            ),
            compiler_params=pltpu.CompilerParams(vmem_limit_bytes=8 * 1024 * 1024),
            name="answer",
        )(asks, cached)
        own = lax.all_to_all(found, "pool", split_axis=0, concat_axis=0, tiled=True)
    else:
        ask = jnp.pad(jnp.concatenate([owners, hit_block]), (0, LANES - 2 * hits))
        ask = jnp.broadcast_to(ask[None, :], (peers, LANES))
        asks = lax.all_to_all(ask, "pool", split_axis=0, concat_axis=0, tiled=True)

        length = suffix_len[0]
        live = lax.iota(jnp.int32, rows) < length
        mine_lat = jnp.where(live[:, None], new_lat, jnp.zeros_like(new_lat))
        mine_rope = jnp.where(live[:, None], new_rope, jnp.zeros_like(new_rope))
        mine_lat = mine_lat.reshape(new_count, 2, half, latent)
        mine_lat = lax.dynamic_index_in_dim(mine_lat, core, axis=1, keepdims=False)
        rope_rows = half * rope_width // latent
        mine_rope = mine_rope.reshape(new_count, 2, rope_rows, latent)
        mine_rope = lax.dynamic_index_in_dim(mine_rope, core, axis=1, keepdims=False)
        every = jnp.concatenate([mine_lat, mine_rope], axis=1)
        bit = peers // 2
        other = lax.ppermute(every, "pool", [(i, i ^ bit) for i in range(peers)])
        asks, every, other = lax.optimization_barrier((asks, every, other))
        every = jnp.concatenate([every, other], axis=0)

        found = pl.pallas_call(
            functools.partial(gather_kernel, hits),
            grid_spec=pltpu.PrefetchScalarGridSpec(
                num_scalar_prefetch=1,
                grid=(1,),
                in_specs=[pl.BlockSpec(memory_space=pltpu.VMEM)],
                out_specs=pl.BlockSpec(memory_space=pltpu.VMEM),
            ),
            out_shape=jax.ShapeDtypeStruct((peers, CAP, depth, LANES), cached.dtype),
            compiler_params=pltpu.CompilerParams(vmem_limit_bytes=16 * 1024 * 1024),
            name="gather_hits",
        )(asks, cached)
        found = found.reshape(peers, CAP * depth, LANES)
        own = lax.all_to_all(found, "pool", split_axis=0, concat_axis=0, tiled=True)
    q_heads = q_lat.transpose(1, 0, 2)
    qr_heads = q_rope.reshape(rows, heads, rope_width).transpose(1, 0, 2)
    group = 8
    tail = pl.pallas_call(
        functools.partial(suffix_kernel, group),
        in_specs=[whole] * 2 + [anywhere] * 2,
        out_specs=whole,
        out_shape=jax.ShapeDtypeStruct((heads, rows, rows), jnp.float32),
        scratch_shapes=[
            pltpu.VMEM(q_heads.shape, q_heads.dtype),
            pltpu.VMEM(qr_heads.shape, qr_heads.dtype),
            pltpu.SemaphoreType.DMA((heads // group, 2)),
        ],
        compiler_params=pltpu.CompilerParams(vmem_limit_bytes=58 * 1024 * 1024),
        cost_estimate=pl.CostEstimate(
            flops=2 * heads * rows * rows * (latent + rope_width),
            bytes_accessed=12 * 2**20,
            transcendentals=0,
        ),
        name="suffix",
    )(new_lat, new_rope.T, q_heads, qr_heads)
    own, tail = lax.optimization_barrier((own, tail))
    sib = lax.ppermute(own, "tp", swap)
    if not two_hops:
        source = new_place // new_count
        differs = source ^ me
        place = ((differs & bit) != 0).astype(jnp.int32)
        bit //= 2
        step = 1
        while bit:
            other = lax.ppermute(every, "pool", [(i, i ^ bit) for i in range(peers)])
            every = jnp.concatenate([every, other], axis=0)
            place = place + ((differs & bit) != 0).astype(jnp.int32) * (1 << step)
            bit //= 2
            step += 1
        chosen = every[place * new_count + new_place % new_count]
        chosen_sib = lax.ppermute(chosen, "tp", swap)
        first = jnp.where(core == 0, chosen, chosen_sib)
        second = jnp.where(core == 0, chosen_sib, chosen)
        written_lat = jnp.concatenate([first[:, :half], second[:, :half]], axis=1)
        written_rope = jnp.concatenate([first[:, half:], second[:, half:]], axis=1).reshape(
            new_place.shape[0], block_len * rope_width
        )

    total = hits * block_len + rows
    flops = 2 * heads * rows * (total * (2 * latent + rope_width) + latent * vhead)
    out_specs = [pl.BlockSpec((rows, group * vhead), lambda i, *_: (0, i))]
    out_shape = [jax.ShapeDtypeStruct((rows, heads * vhead), jnp.bfloat16)]
    if two_hops:
        slots = new_place.shape[0]
        for shape in ((slots, block_len, latent), (slots, block_len * rope_width)):
            out_specs.append(whole)
            out_shape.append(jax.ShapeDtypeStruct(shape, new_lat.dtype))
    streamed = [
        pl.BlockSpec((group,) + x.shape[1:], lambda i, *_: (i, 0, 0))
        for x in (q_heads, qr_heads, tail, w_uv)
    ]
    attn_out, *written = pl.pallas_call(
        functools.partial(attend_kernel, block_len, hits),
        grid_spec=pltpu.PrefetchScalarGridSpec(
            num_scalar_prefetch=1,
            grid=(heads // group,),
            in_specs=[whole] * 3 + streamed,
            out_specs=out_specs,
            scratch_shapes=[
                pltpu.VMEM((total, latent), jnp.bfloat16),
                pltpu.VMEM((hits * block_len, rope_width), jnp.bfloat16),
            ],
        ),
        out_shape=out_shape,
        compiler_params=pltpu.CompilerParams(vmem_limit_bytes=52 * 1024 * 1024),
        cost_estimate=pl.CostEstimate(
            flops=flops, bytes_accessed=10 * 2**20, transcendentals=heads * rows * total
        ),
        name="attend",
    )(jnp.concatenate([owners, suffix_len]), own, sib, new_lat, q_heads, qr_heads, tail, w_uv)
    if two_hops:
        written_lat, written_rope = written
    return (attn_out, written_lat, written_rope)


def solution(mesh):
    return jax.shard_map(
        local,
        mesh=mesh,
        in_specs=(
            P(("groups", "pool"), "tp", None),
            P(("groups", "pool"), "tp"),
            P(("groups", "pool"), None),
            P(("groups", "pool"), None),
            P(("groups", "pool"), None, None),
            P(("groups", "pool"), None),
            P(("groups", "pool")),
            P(("groups", "pool"), None),
            P(("groups", "pool")),
            P(("groups", "pool")),
            P("tp", None, None),
        ),
        out_specs=(
            P(("groups", "pool"), "tp"),
            P(("groups", "pool"), None, None),
            P(("groups", "pool"), None),
        ),
        check_vma=False,
    )
```

```python
import functools
import math

import jax
import jax.numpy as jnp
from jax import lax
from jax.experimental import pallas as pl
from jax.experimental.pallas import tpu as pltpu
from jax.sharding import PartitionSpec as P

CAP = 2
LANES = 128
softmax_scale = 1.0 / math.sqrt(192.0)
exp2_scale = softmax_scale / math.log(2.0)


def gather_kernel(hits, asks, pool_ref, out_ref):
    me = lax.axis_index("pool")

    def body(r, carry):
        rank = jnp.int32(0)
        wanted = [jnp.int32(0)] * CAP
        for k in range(hits):
            mine = (asks[r, k] == me).astype(jnp.int32)
            for s in range(CAP):
                wanted[s] = jnp.where((rank == s) & (mine == 1), asks[r, hits + k], wanted[s])
            rank = rank + mine
        for s in range(CAP):
            out_ref[r, s] = pool_ref[wanted[s]]
        return carry

    lax.fori_loop(0, out_ref.shape[0], body, 0)


def ask_kernel(block_len, *refs):
    sources, out_ref, held = refs[:6], refs[6], refs[7:13]
    tokens, rows32, sems = refs[13:]
    copies = [
        pltpu.make_async_copy(source, dest, sems.at[i])
        for i, (source, dest) in enumerate(zip(sources, held))
    ]
    for copy in copies:
        copy.start()
    for copy in copies:
        copy.wait()
    hit_block, hit_owner, length, new_place, lat_ref, rope_ref = held
    core = lax.axis_index("tp")
    pieces = out_ref.shape[0]
    latent = lat_ref.shape[1]
    tiles = latent // LANES
    half = block_len // 2
    part = half // (pieces // tiles)
    new_count = lat_ref.shape[0] // block_len
    hits = hit_block.shape[0]
    pairs = half // 2 // pieces

    lane = lax.broadcasted_iota(jnp.int32, (1, LANES), 1)
    ask = jnp.zeros((1, LANES), jnp.int32)
    for k in range(hits):
        ask = jnp.where(lane == k, hit_owner[k], ask)
        ask = jnp.where(lane == hits + k, hit_block[k], ask)
    for s in range(new_count):
        ask = jnp.where(lane == 2 * hits + s, new_place[s], ask)
    ask = ask.astype(jnp.float32)

    turned = rope_ref[...].astype(jnp.float32).T
    token_keep = lax.broadcasted_iota(jnp.int32, turned.shape, 0) < length[0]
    tokens[: turned.shape[0], :] = jnp.where(token_keep, turned, 0.0)
    for b in range(new_count):
        base = b * block_len + core * half
        at = pl.multiple_of(base, half)
        keep = lax.broadcasted_iota(jnp.int32, (half, latent), 0) + base < length[0]
        lat = jnp.where(keep, lat_ref[pl.ds(at, half), :].astype(jnp.float32), 0.0)
        lat = lat.astype(out_ref.dtype)
        for j in range(pieces):
            u, t = j // tiles, j % tiles
            out_ref[j, b * part : (b + 1) * part, :] = lat[
                u * part : (u + 1) * part, t * LANES : (t + 1) * LANES
            ]
        even = tokens[pl.ds(at, half // 2, stride=2), :]
        odd = tokens[pl.ds(at + 1, half // 2, stride=2), :]
        paired = jnp.concatenate([even, odd], axis=1)
        for j in range(pieces):
            for p in range(pairs):
                row = p * new_count + b
                g = j * pairs + p
                rows32[j, row : row + 1, :] = paired[g : g + 1]
    filled = pairs * new_count
    for j in range(pieces):
        rows32[j, filled:8, :] = jnp.zeros((8 - filled, LANES), jnp.float32)
        rows32[j, 8:16, :] = jnp.broadcast_to(ask, (8, LANES))
        out_ref[j, new_count * part :, :] = rows32[j].astype(out_ref.dtype)


def answer_kernel(hits, new_count, asks_ref, pool_ref, out_any, out_ref, rows32, ids_vec, ids, sem, out_sems):
    me = lax.axis_index("pool")
    peers, depth = out_ref.shape[0], pool_ref.shape[1]
    tail = asks_ref.shape[1] - 16
    part = tail // new_count
    for r in range(peers):
        tile = asks_ref[r, tail:, :].astype(jnp.float32)
        rows32[r] = tile
        ids_vec[r : r + 1, :] = tile[8:9].astype(jnp.int32)
    copy = pltpu.make_async_copy(ids_vec, ids, sem)
    copy.start()
    copy.wait()
    pairs_row = lax.broadcasted_iota(jnp.int32, (8, LANES), 0)

    def body(r, carry):
        rank = jnp.int32(0)
        wanted = [jnp.int32(0)] * CAP
        for k in range(hits):
            mine = (ids[r, k] == me).astype(jnp.int32)
            for s in range(CAP):
                wanted[s] = jnp.where((rank == s) & (mine == 1), ids[r, hits + k], wanted[s])
            rank = rank + mine
        for s in range(CAP):
            out_ref[r, s * depth : (s + 1) * depth, :] = pool_ref[wanted[s]]
        base = CAP * depth
        merged = jnp.zeros((8, LANES), jnp.float32)
        for s in range(new_count):
            place = ids[r, 2 * hits + s]
            source, block = place // new_count, place % new_count
            out_ref[r, base + s * part : base + (s + 1) * part, :] = asks_ref[
                source, pl.ds(pl.multiple_of(block * part, part), part), :
            ]
            tile = rows32[source, 0:8, :]
            shifted = tile
            for move in range(1, new_count):
                up = pltpu.roll(tile, 8 - move, 0)
                down = pltpu.roll(tile, move, 0)
                shifted = jnp.where(block - s == move, up, shifted)
                shifted = jnp.where(s - block == move, down, shifted)
            merged = jnp.where(pairs_row % new_count == s, shifted, merged)
        both = jnp.concatenate([merged, jnp.zeros((8, LANES), jnp.float32)], axis=0)
        out_ref[r, base + tail :, :] = both.astype(out_ref.dtype)
        leave(r).start()
        return carry

    def leave(r):
        return pltpu.make_async_copy(out_ref.at[r], out_any.at[r], out_sems.at[r])

    lax.fori_loop(0, peers, body, 0)
    for r in range(peers):
        leave(r).wait()


def write_back(block_len, base, own_ref, sib_ref, lat_ref, rope_ref):
    core = lax.axis_index("tp")
    pieces = own_ref.shape[0]
    slots, _, latent = lat_ref.shape
    tiles = latent // LANES
    half = block_len // 2
    part = half // (pieces // tiles)
    pairs = half // 2 // pieces
    sides = []
    for side, ref in enumerate((own_ref, sib_ref)):
        start = pl.multiple_of((core if side == 0 else 1 - core) * half, half)
        row = []
        for j in range(pieces):
            u, t = j // tiles, j % tiles
            for s in range(slots):
                lat_ref[s, pl.ds(start + u * part, part), t * LANES : (t + 1) * LANES] = ref[
                    j, base + s * part : base + (s + 1) * part, :
                ]
            tile = ref[j, base + slots * part :, :].astype(jnp.float32)
            for p in range(pairs):
                row.append(tile[p * slots : (p + 1) * slots])
        sides.append(jnp.concatenate(row, axis=1))
    first = jnp.where(core == 0, sides[0], sides[1])
    second = jnp.where(core == 0, sides[1], sides[0])
    rope_ref[...] = jnp.concatenate([first, second], axis=1).astype(rope_ref.dtype)


def suffix_kernel(group, lat_ref, rope_ref, *refs):
    sources, out_ref, held, sems = refs[:2], refs[2], refs[3:5], refs[5]
    q_ref, qr_ref = held
    heads, rows, latent = q_ref.shape
    steps = heads // group

    def arrive(g, a):
        at = pl.ds(g * group, group)
        return pltpu.make_async_copy(sources[a].at[at], held[a].at[at], sems.at[g, a])

    for g in range(steps):
        arrive(g, 0).start()
        arrive(g, 1).start()
    position = lax.broadcasted_iota(jnp.int32, (group, rows, rows), 1)
    key_at = lax.broadcasted_iota(jnp.int32, (group, rows, rows), 2)
    for g in range(steps):
        arrive(g, 0).wait()
        arrive(g, 1).wait()
        at = slice(g * group, (g + 1) * group)
        q = q_ref[at].reshape(group * rows, latent)
        qr = qr_ref[at].reshape(group * rows, qr_ref.shape[2])
        scores = lax.dot_general(
            q, lat_ref[...], (((1,), (1,)), ((), ())), preferred_element_type=jnp.float32
        )
        scores = scores + jnp.dot(qr, rope_ref[...], preferred_element_type=jnp.float32)
        out_ref[at] = jnp.where(key_at <= position, scores.reshape(group, rows, rows), -1e30)


def attend_kernel(
    block_len, hits, numbers, own_ref, sib_ref, new_lat_ref, q_ref, qr_ref, tail_ref, w_ref, *refs
):
    out_ref, *written = refs[:-2]
    keys, rope = refs[-2:]
    group, rows, latent = q_ref.shape
    rope_width = qr_ref.shape[2]
    width = w_ref.shape[2]
    half = block_len // 2
    quarter = half // 2
    prefix = hits * block_len
    tiles = latent // LANES
    depth = tiles * half + quarter

    @pl.when(pl.program_id(0) == 0)
    def _():
        for k in range(hits):
            owner = numbers[k]
            rank = jnp.int32(0)
            for j in range(k):
                rank = rank + (numbers[j] == owner).astype(jnp.int32)
            slot = pl.multiple_of(jnp.minimum(rank, CAP - 1) * depth, 16)
            for side, ref in enumerate((own_ref, sib_ref)):
                block = ref.at[owner, pl.ds(slot, depth), :]
                base = k * block_len + side * half
                for t in range(tiles):
                    keys[base : base + half, t * LANES : (t + 1) * LANES] = block[
                        t * half : (t + 1) * half, :
                    ]
                packed = block[tiles * half : tiles * half + quarter, :]
                rope[base : base + quarter, :] = packed[:, :rope_width]
                rope[base + quarter : base + half, :] = packed[:, rope_width:]
        keys[prefix:, :] = new_lat_ref[...]
        if written:
            write_back(block_len, depth * CAP, own_ref, sib_ref, *written)

    contract = (((1,), (1,)), ((), ()))
    live = lax.broadcasted_iota(jnp.int32, (rows, width), 0) < numbers[hits]
    some = 4

    def score(i):
        at = slice(i * some, (i + 1) * some)
        q = q_ref[at].reshape(some * rows, latent)
        qr = qr_ref[at].reshape(some * rows, rope_width)
        scores = lax.dot_general(q, keys[:prefix, :], contract, preferred_element_type=jnp.float32)
        scores = scores + lax.dot_general(
            qr, rope[...], contract, preferred_element_type=jnp.float32
        )
        return jnp.concatenate([scores, tail_ref[at].reshape(some * rows, rows)], axis=1)

    def finish(i, scores):
        top = jnp.max(scores, axis=1, keepdims=True)
        parts = jnp.exp2((scores - top) * exp2_scale)
        norm = 1.0 / jnp.sum(parts, axis=1, keepdims=True)
        weights = (parts * norm).astype(jnp.bfloat16)
        context = jnp.dot(weights, keys[...], preferred_element_type=jnp.float32)
        context = context.astype(jnp.bfloat16)
        for h in range(some):
            value = jnp.dot(
                context[h * rows : (h + 1) * rows],
                w_ref[i * some + h],
                preferred_element_type=jnp.float32,
            )
            lanes = slice((i * some + h) * width, (i * some + h + 1) * width)
            out_ref[:, lanes] = jnp.where(live, value, 0.0).astype(out_ref.dtype)

    scores = score(0)
    for i in range(group // some):
        later = score(i + 1) if (i + 1) * some < group else None
        finish(i, scores)
        scores = later


def local(
    q_lat,
    q_rope,
    new_lat,
    new_rope,
    pool_lat,
    pool_rope,
    hit_block,
    hit_owner,
    suffix_len,
    new_place,
    w_uv,
):
    peers = lax.axis_size("pool")
    me = lax.axis_index("pool")
    core = lax.axis_index("tp")
    cores = lax.axis_size("tp")
    assert cores == 2
    hits = hit_block.shape[0]
    blocks, block_len, latent = pool_lat.shape
    rows, rope_width = new_rope.shape
    half = block_len // 2
    quarter = half // 2
    tiles = latent // LANES
    heads = q_lat.shape[1]
    vhead = w_uv.shape[2]
    new_count = rows // block_len
    swap = [(0, 1), (1, 0)]

    owners = hit_owner[:, 0]
    whole = pl.BlockSpec(memory_space=pltpu.VMEM)
    anywhere = pl.BlockSpec(memory_space=pl.ANY)
    part = half * tiles // peers
    two_hops = peers % tiles == 0 and part % 16 == 0 and half % (2 * peers) == 0

    lat_half = lax.dynamic_slice_in_dim(pool_lat, core * half, half, axis=1)
    lat_half = lat_half.reshape(blocks, half, tiles, LANES).transpose(0, 2, 1, 3)
    rope_half = lax.dynamic_slice_in_dim(
        pool_rope, core * half * rope_width, half * rope_width, axis=1
    )
    rope_half = rope_half.reshape(blocks, 2, quarter, rope_width).transpose(0, 2, 1, 3)
    cached = jnp.concatenate(
        [
            lat_half.reshape(blocks, tiles * half, LANES),
            rope_half.reshape(blocks, quarter, 2 * rope_width),
        ],
        axis=1,
    )
    depth = cached.shape[1]

    if two_hops:
        asked = pl.pallas_call(
            functools.partial(ask_kernel, block_len),
            in_specs=[anywhere] * 6,
            out_specs=whole,
            scratch_shapes=[
                pltpu.SMEM((hits,), jnp.int32),
                pltpu.SMEM((hits,), jnp.int32),
                pltpu.SMEM((1,), jnp.int32),
                pltpu.SMEM(new_place.shape, jnp.int32),
                pltpu.VMEM((rows, latent), new_lat.dtype),
                pltpu.VMEM((rope_width, rows), new_rope.dtype),
                pltpu.VMEM((rows + 8, rope_width), jnp.float32),
                pltpu.VMEM((peers, 16, LANES), jnp.float32),
                pltpu.SemaphoreType.DMA((6,)),
            ],
            out_shape=jax.ShapeDtypeStruct((peers, new_count * part + 16, LANES), new_lat.dtype),
            compiler_params=pltpu.CompilerParams(vmem_limit_bytes=60 * 1024 * 1024),
            name="ask",
        )(hit_block, owners, suffix_len, new_place, new_lat, new_rope.T)
        asks = lax.all_to_all(asked, "pool", split_axis=0, concat_axis=0, tiled=True)
        found = pl.pallas_call(
            functools.partial(answer_kernel, hits, new_count),
            in_specs=[whole] * 2,
            out_specs=anywhere,
            scratch_shapes=[
                pltpu.VMEM((peers, CAP * depth + new_count * part + 16, LANES), cached.dtype),
                pltpu.VMEM((peers, 16, LANES), jnp.float32),
                pltpu.VMEM((peers, LANES), jnp.int32),
                pltpu.SMEM((peers, LANES), jnp.int32),
                pltpu.SemaphoreType.DMA,
                pltpu.SemaphoreType.DMA((peers,)),
            ],
            out_shape=jax.ShapeDtypeStruct(
                (peers, CAP * depth + new_count * part + 16, LANES), cached.dtype
            ),
            compiler_params=pltpu.CompilerParams(vmem_limit_bytes=8 * 1024 * 1024),
            name="answer",
        )(asks, cached)
        own = lax.all_to_all(found, "pool", split_axis=0, concat_axis=0, tiled=True)
    else:
        ask = jnp.pad(jnp.concatenate([owners, hit_block]), (0, LANES - 2 * hits))
        ask = jnp.broadcast_to(ask[None, :], (peers, LANES))
        asks = lax.all_to_all(ask, "pool", split_axis=0, concat_axis=0, tiled=True)

        length = suffix_len[0]
        live = lax.iota(jnp.int32, rows) < length
        mine_lat = jnp.where(live[:, None], new_lat, jnp.zeros_like(new_lat))
        mine_rope = jnp.where(live[:, None], new_rope, jnp.zeros_like(new_rope))
        mine_lat = mine_lat.reshape(new_count, 2, half, latent)
        mine_lat = lax.dynamic_index_in_dim(mine_lat, core, axis=1, keepdims=False)
        rope_rows = half * rope_width // latent
        mine_rope = mine_rope.reshape(new_count, 2, rope_rows, latent)
        mine_rope = lax.dynamic_index_in_dim(mine_rope, core, axis=1, keepdims=False)
        every = jnp.concatenate([mine_lat, mine_rope], axis=1)
        bit = peers // 2
        other = lax.ppermute(every, "pool", [(i, i ^ bit) for i in range(peers)])
        asks, every, other = lax.optimization_barrier((asks, every, other))
        every = jnp.concatenate([every, other], axis=0)

        found = pl.pallas_call(
            functools.partial(gather_kernel, hits),
            grid_spec=pltpu.PrefetchScalarGridSpec(
                num_scalar_prefetch=1,
                grid=(1,),
                in_specs=[pl.BlockSpec(memory_space=pltpu.VMEM)],
                out_specs=pl.BlockSpec(memory_space=pltpu.VMEM),
            ),
            out_shape=jax.ShapeDtypeStruct((peers, CAP, depth, LANES), cached.dtype),
            compiler_params=pltpu.CompilerParams(vmem_limit_bytes=16 * 1024 * 1024),
            name="gather_hits",
        )(asks, cached)
        found = found.reshape(peers, CAP * depth, LANES)
        own = lax.all_to_all(found, "pool", split_axis=0, concat_axis=0, tiled=True)
    q_heads = q_lat.transpose(1, 0, 2)
    qr_heads = q_rope.reshape(rows, heads, rope_width).transpose(1, 0, 2)
    group = 8
    tail = pl.pallas_call(
        functools.partial(suffix_kernel, group),
        in_specs=[whole] * 2 + [anywhere] * 2,
        out_specs=whole,
        out_shape=jax.ShapeDtypeStruct((heads, rows, rows), jnp.float32),
        scratch_shapes=[
            pltpu.VMEM(q_heads.shape, q_heads.dtype),
            pltpu.VMEM(qr_heads.shape, qr_heads.dtype),
            pltpu.SemaphoreType.DMA((heads // group, 2)),
        ],
        compiler_params=pltpu.CompilerParams(vmem_limit_bytes=58 * 1024 * 1024),
        cost_estimate=pl.CostEstimate(
            flops=2 * heads * rows * rows * (latent + rope_width),
            bytes_accessed=12 * 2**20,
            transcendentals=0,
        ),
        name="suffix",
    )(new_lat, new_rope.T, q_heads, qr_heads)
    own, tail = lax.optimization_barrier((own, tail))
    sib = lax.ppermute(own, "tp", swap)
    if not two_hops:
        source = new_place // new_count
        differs = source ^ me
        place = ((differs & bit) != 0).astype(jnp.int32)
        bit //= 2
        step = 1
        while bit:
            other = lax.ppermute(every, "pool", [(i, i ^ bit) for i in range(peers)])
            every = jnp.concatenate([every, other], axis=0)
            place = place + ((differs & bit) != 0).astype(jnp.int32) * (1 << step)
            bit //= 2
            step += 1
        chosen = every[place * new_count + new_place % new_count]
        chosen_sib = lax.ppermute(chosen, "tp", swap)
        first = jnp.where(core == 0, chosen, chosen_sib)
        second = jnp.where(core == 0, chosen_sib, chosen)
        written_lat = jnp.concatenate([first[:, :half], second[:, :half]], axis=1)
        written_rope = jnp.concatenate([first[:, half:], second[:, half:]], axis=1).reshape(
            new_place.shape[0], block_len * rope_width
        )

    total = hits * block_len + rows
    flops = 2 * heads * rows * (total * (2 * latent + rope_width) + latent * vhead)
    out_specs = [pl.BlockSpec((rows, group * vhead), lambda i, *_: (0, i))]
    out_shape = [jax.ShapeDtypeStruct((rows, heads * vhead), jnp.bfloat16)]
    if two_hops:
        slots = new_place.shape[0]
        for shape in ((slots, block_len, latent), (slots, block_len * rope_width)):
            out_specs.append(whole)
            out_shape.append(jax.ShapeDtypeStruct(shape, new_lat.dtype))
    streamed = [
        pl.BlockSpec((group,) + x.shape[1:], lambda i, *_: (i, 0, 0))
        for x in (q_heads, qr_heads, tail, w_uv)
    ]
    attn_out, *written = pl.pallas_call(
        functools.partial(attend_kernel, block_len, hits),
        grid_spec=pltpu.PrefetchScalarGridSpec(
            num_scalar_prefetch=1,
            grid=(heads // group,),
            in_specs=[whole] * 3 + streamed,
            out_specs=out_specs,
            scratch_shapes=[
                pltpu.VMEM((total, latent), jnp.bfloat16),
                pltpu.VMEM((hits * block_len, rope_width), jnp.bfloat16),
            ],
        ),
        out_shape=out_shape,
        compiler_params=pltpu.CompilerParams(vmem_limit_bytes=52 * 1024 * 1024),
        cost_estimate=pl.CostEstimate(
            flops=flops, bytes_accessed=10 * 2**20, transcendentals=heads * rows * total
        ),
        name="attend",
    )(jnp.concatenate([owners, suffix_len]), own, sib, new_lat, q_heads, qr_heads, tail, w_uv)
    if two_hops:
        written_lat, written_rope = written
    return (attn_out, written_lat, written_rope)


def solution(mesh):
    return jax.shard_map(
        local,
        mesh=mesh,
        in_specs=(
            P(("groups", "pool"), "tp", None),
            P(("groups", "pool"), "tp"),
            P(("groups", "pool"), None),
            P(("groups", "pool"), None),
            P(("groups", "pool"), None, None),
            P(("groups", "pool"), None),
            P(("groups", "pool")),
            P(("groups", "pool"), None),
            P(("groups", "pool")),
            P(("groups", "pool")),
            P("tp", None, None),
        ),
        out_specs=(
            P(("groups", "pool"), "tp"),
            P(("groups", "pool"), None, None),
            P(("groups", "pool"), None),
        ),
        check_vma=False,
    )
```
